256 devices in a mesh: wide: 32 (over z, y_hi, core), narrow: 8 (over y_lo, x).
Axes of the slice: x: 4, y: 4 (y_hi: 2, y_lo: 2; y = y_hi * 2 + y_lo), z: 8, core: 2. Of those that a mesh axis runs over, the one named last changes fastest.
Arguments:
- buoyancy: float32 [512, 512, 128], P('wide', 'narrow'), may hold values from -6 to 6
- velocity_x: float32 [512, 512, 128], P('wide', 'narrow'), may hold values from -0.0078125 to 0.0078125
- velocity_y: float32 [512, 512, 128], P('wide', 'narrow'), may hold values from -0.0078125 to 0.0078125
- velocity_z: float32 [512, 512, 128], P('wide', 'narrow'), may hold values from -0.0078125 to 0.0078125
- inverse_blocks: bfloat16 [256, 256, 128, 128], P('wide', 'narrow'), may hold values from -1 to 2, as said below
Outputs:
- new_buoyancy: float32 [512, 512, 128], P('wide', 'narrow')
The draws below stay inside these ranges and needn't reach their ends.
Inputs may be any that keep to these rules, and one draw needn't show every extreme that they name: `inverse_blocks`: dense 128 x 128 blocks, one for each pair of x and y mode numbers.
All inputs are finite; a program needn't handle non-finite values.
Results may differ from the reference program's by a relative error of at most 0.0029.
Values sent between devices are 32-bit elements; how exact they have to be, the bound alone decides.
A program may use at most 128 MiB of HBM per device.

```python
import math
import jax
import jax.numpy as jnp
from jax import lax

NX = 512
NY = 512
NZ = 128
MX = 768
MY = 768
MZ = 192


def draw_inverse_blocks(key, part):
    key = jax.random.fold_in(key, 7)
    noise_key, diag_key = jax.random.split(key)
    noise = jnp.clip(jax.random.normal(noise_key, (NX // 2, NY // 2, NZ, NZ), jnp.float32), -5.0, 5.0)
    noise = noise * (0.6 / math.sqrt(NZ))
    diagonal = jax.random.uniform(diag_key, (NX // 2, NY // 2, NZ, 1), jnp.float32, 0.5, 1.5)
    identity = jnp.eye(NZ, dtype=jnp.float32)
    return (noise + diagonal * identity).astype(jnp.bfloat16)


def level_of(key, shape, cuts, least, largest):
    gain = 1.0
    for position, blocks in cuts:
        draws = jax.random.uniform(jax.random.fold_in(jax.random.fold_in(key, 6), position), (blocks,), jnp.float32, least / len(cuts), largest / len(cuts))
        gain = gain * jnp.repeat(jnp.exp(draws), shape[position] // blocks).reshape((-1,) + (1,) * (len(shape) - 1 - position))
    return gain


def centred(key, extent, spread, most, pieces=(), kind=jnp.bfloat16):
    drawn = spread * jax.random.normal(key, extent, jnp.float32)
    if pieces:
        drawn = drawn * level_of(key, extent, pieces, -0.22, 0.18)
    return jnp.clip(drawn, -most, most).astype(kind)


def setup_inputs(seed: int = 0) -> dict:
    splits = jax.random.split(jax.random.key(seed), 6)
    return {
        "buoyancy": centred(splits[0], (NX, NY, NZ), 1.0, 6.0, ((0, 32), (1, 8)), jnp.float32),
        "velocity_x": centred(splits[1], (NX, NY, NZ), ((8 / (NX * NY * NZ)) ** 0.5), 0.0078125, ((0, 32), (1, 8)), jnp.float32),
        "velocity_y": centred(splits[2], (NX, NY, NZ), ((8 / (NX * NY * NZ)) ** 0.5), 0.0078125, ((0, 32), (1, 8)), jnp.float32),
        "velocity_z": centred(splits[3], (NX, NY, NZ), ((8 / (NX * NY * NZ)) ** 0.5), 0.0078125, ((0, 32), (1, 8)), jnp.float32),
        "inverse_blocks": draw_inverse_blocks(jax.random.fold_in(splits[5], 71), 0),
    }


def cheb_table(n_coef, n_grid, dtype):
    orders = jnp.arange(n_coef)
    points = jnp.arange(n_grid)
    index_grid = (orders[:, None] * (2 * points[None, :] + 1)) % (4 * n_grid)
    return jnp.cos(index_grid.astype(dtype) * (math.pi / (2 * n_grid)))


def cheb_inverse(n_coef, n_grid, dtype):
    orders = jnp.arange(n_coef)
    weight = jnp.where(orders == 0, 1.0 / n_grid, 2.0 / n_grid).astype(dtype)
    return cheb_table(n_coef, n_grid, dtype).T * weight[None, :]


def cheb_slope(n_coef, dtype):
    rows = jnp.arange(n_coef)[:, None]
    cols = jnp.arange(n_coef)[None, :]
    inside = (cols > rows) & ((cols - rows) % 2 == 1)
    factor = jnp.where(rows == 0, 1.0, 2.0) * cols
    return jnp.where(inside, factor, 0.0).astype(dtype)


def fourier_grid(values, axis_pos, n_grid):
    values = jnp.moveaxis(values, axis_pos, -1)
    half = values.shape[-1] // 2
    modes = jnp.arange(half)
    scale = jnp.where(modes == 0, 1.0, 0.5).astype(values.dtype)
    keep = jnp.where(modes == 0, 0.0, 1.0).astype(values.dtype)
    real_part = values[..., 0::2] * scale
    imag_part = -values[..., 1::2] * scale * keep
    spectrum = lax.complex(real_part, imag_part)
    widths = [(0, 0)] * (spectrum.ndim - 1) + [(0, n_grid // 2 + 1 - half)]
    spectrum = jnp.pad(spectrum, widths)
    result = jnp.fft.irfft(spectrum, n=n_grid, axis=-1) * n_grid
    return jnp.moveaxis(result, -1, axis_pos)


def fourier_coef(values, axis_pos, n_coef):
    values = jnp.moveaxis(values, axis_pos, -1)
    n_grid = values.shape[-1]
    half = n_coef // 2
    spectrum = jnp.fft.rfft(values, axis=-1)[..., :half]
    modes = jnp.arange(half)
    weight = jnp.where(modes == 0, 1.0 / n_grid, 2.0 / n_grid).astype(values.dtype)
    keep = jnp.where(modes == 0, 0.0, 1.0).astype(values.dtype)
    cosines = jnp.real(spectrum) * weight
    sines = -jnp.imag(spectrum) * weight * keep
    result = jnp.stack([cosines, sines], -1).reshape(values.shape[:-1] + (n_coef,))
    return jnp.moveaxis(result, -1, axis_pos)


def fourier_slope(values, axis_pos):
    values = jnp.moveaxis(values, axis_pos, -1)
    half = values.shape[-1] // 2
    modes = jnp.arange(half).astype(values.dtype)
    cosines = values[..., 0::2]
    sines = values[..., 1::2]
    result = jnp.stack([modes * sines, -modes * cosines], -1).reshape(values.shape)
    return jnp.moveaxis(result, -1, axis_pos)


def reference(buoyancy, velocity_x, velocity_y, velocity_z, inverse_blocks):
    dtype = buoyancy.dtype
    z_forward = cheb_table(NZ, MZ, dtype)
    z_backward = cheb_inverse(NZ, MZ, dtype)
    z_slope = cheb_slope(NZ, dtype)

    def to_grid(coefs):
        along_z = jnp.einsum('xyn,nq->xyq', coefs, z_forward, precision=lax.Precision.HIGHEST)
        along_y = fourier_grid(along_z, 1, MY)
        return fourier_grid(along_y, 0, MX)

    def to_coef(values):
        along_x = fourier_coef(values, 0, NX)
        along_y = fourier_coef(along_x, 1, NY)
        return jnp.einsum('xyq,qn->xyn', along_y, z_backward, precision=lax.Precision.HIGHEST)

    buoy_grid = to_grid(buoyancy)
    term_x = fourier_slope(to_coef(to_grid(velocity_x) * buoy_grid), 0)
    term_y = fourier_slope(to_coef(to_grid(velocity_y) * buoy_grid), 1)
    flux_z = to_coef(to_grid(velocity_z) * buoy_grid)
    term_z = jnp.einsum('xyp,np->xyn', flux_z, z_slope, precision=lax.Precision.HIGHEST)
    nonlinear = term_x + term_y + term_z
    right_side = (buoyancy - (4.0 / NX) * nonlinear).astype(jnp.bfloat16)
    right_side = lax.optimization_barrier(right_side)
    grouped = right_side.reshape(NX // 2, 2, NY // 2, 2, NZ)

    def solve_row(pair):
        blocks_row, columns = pair
        return jnp.einsum('yin,aybn->aybi', blocks_row.astype(jnp.float32), columns.astype(jnp.float32))

    solved = lax.map(solve_row, (inverse_blocks, grouped))
    return solved.reshape(NX, NY, NZ)
```

```python
import functools

import jax
import jax.numpy as jnp
import ml_dtypes
import numpy as np
from jax import lax
from jax.experimental import pallas as pl
from jax.experimental.pallas import tpu as pltpu
from jax.sharding import PartitionSpec as P

NX = 512
NY = 512
NZ = 128
MX = 768
MY = 768
MZ = 192
W = 32
N = 8
XL = NX // W
YL = NY // N
QL = MZ // W
PL = MX // N
PAIRS = QL // 2
F32 = jnp.float32
BF16 = jnp.bfloat16
MESH = pl.DeviceIdType.MESH


def fourier_table(n_coef, n_grid):
    index = np.arange(n_coef)
    phase = (index[:, None] // 2 * np.arange(n_grid)[None, :] % n_grid) * (2.0 * np.pi / n_grid)
    return np.where((index % 2 == 0)[:, None], np.cos(phase), np.sin(phase))


def fourier_inverse(n_coef, n_grid):
    index = np.arange(n_coef)
    modes = index // 2
    weight = np.where(modes == 0, np.where(index % 2 == 0, 1.0 / n_grid, 0.0), 2.0 / n_grid)
    return fourier_table(n_coef, n_grid).T * weight[None, :]


def fourier_inverse_slope(n_coef, n_grid):
    plain = fourier_inverse(n_coef, n_grid)
    modes = np.arange(n_coef // 2)[None, :]
    result = np.empty_like(plain)
    result[:, 0::2] = modes * plain[:, 1::2]
    result[:, 1::2] = -modes * plain[:, 0::2]
    return result


def cheb_table(n_coef, n_grid):
    orders = np.arange(n_coef)
    points = np.arange(n_grid)
    index_grid = orders[:, None] * (2 * points[None, :] + 1) % (4 * n_grid)
    return np.cos(index_grid * (np.pi / (2 * n_grid)))


def cheb_inverse(n_coef, n_grid):
    weight = np.where(np.arange(n_coef) == 0, 1.0 / n_grid, 2.0 / n_grid)
    return cheb_table(n_coef, n_grid).T * weight[None, :]


def cheb_slope(n_coef):
    rows = np.arange(n_coef)[:, None]
    cols = np.arange(n_coef)[None, :]
    inside = (cols > rows) & ((cols - rows) % 2 == 1)
    return np.where(inside, np.where(rows == 0, 1.0, 2.0) * cols, 0.0)


def split_table(table):
    high = table.astype(np.float32).astype(ml_dtypes.bfloat16)
    low = (table - high.astype(np.float64)).astype(np.float32).astype(ml_dtypes.bfloat16)
    return np.stack([high, low])


@functools.cache
def tables():
    z_forward = cheb_table(NZ, MZ).T.reshape(W, QL, NZ).transpose(1, 0, 2).reshape(MZ, NZ)
    x_forward = fourier_table(NX, MX).T
    y_forward = fourier_table(NY, MY)
    y_backward = fourier_inverse(NY, MY)
    y_slope = fourier_inverse_slope(NY, MY)
    x_backward = fourier_inverse(NX, MX).T
    x_slope = fourier_inverse_slope(NX, MX).T
    plain = cheb_inverse(NZ, MZ)
    sloped = plain @ cheb_slope(NZ).T
    sides = []
    for parity in range(2):
        blocks = []
        for half in range(2):
            parts = []
            for source in (plain, sloped):
                by_chunk = source.reshape(W, PAIRS, 2, NZ)[:, :, half ^ parity]
                parts.append(by_chunk.transpose(2, 1, 0).reshape(NZ, PAIRS * W))
            parts.append(np.zeros((NZ, 256 - 2 * PAIRS * W)))
            blocks.append(np.concatenate(parts, axis=1))
        sides.append(np.concatenate(blocks, axis=0))
    z_backward = np.stack(sides)
    return [
        split_table(t)
        for t in (z_forward, x_forward, y_forward, y_backward, y_slope, x_backward, x_slope, z_backward)
    ]


def halves(value):
    high = value.astype(BF16)
    return high, (value - high.astype(F32)).astype(BF16)


def dot(a, b, dims=((1,), (0,))):
    return lax.dot_general(a, b, (dims, ((), ())), preferred_element_type=F32)


def dot3(a_high, a_low, b_high, b_low):
    return dot(a_high, b_high) + dot(a_low, b_high) + dot(a_high, b_low)


def rows(start, size):
    return pl.ds(pl.multiple_of(start, 16), size)


def kernel(
    vx_ref, vy_ref, vz_ref, b_ref, zf, zb, xf_hbm, yf_hbm, yb_hbm, ys_hbm, xb_hbm, xs_hbm,
    out_ref,
    send1, recv1, send2, recv2, send3, recv3, send4, recv4,
    xf, yf, yb, ys, xb, xs,
    xh, xl, yh, yl, gh, gl, bh, bl, zh, zl,
    table_sem, s1, r1, s2, r2, s3, r3, s4, r4,
):
    w = lax.axis_index("wide")
    n = lax.axis_index("narrow")
    across = lax.rem(n + 4, N)
    parity = lax.rem(n, 2)
    z_pos, rest = w // 4, lax.rem(w, 4)
    y_pos, x_pos = n // 4, lax.rem(n, 4)

    def wide_peer(k):
        return lax.rem(z_pos + k // 4, 8) * 4 + lax.rem(rest + lax.rem(k, 4), 4)

    def narrow_peer(k):
        return lax.rem(y_pos + k // 4, 2) * 4 + lax.rem(x_pos + lax.rem(k, 4), 4)

    table_copies = [
        pltpu.make_async_copy(hbm, vmem, table_sem.at[i])
        for i, (hbm, vmem) in enumerate(
            ((xf_hbm, xf), (yf_hbm, yf), (yb_hbm, yb), (ys_hbm, ys), (xb_hbm, xb), (xs_hbm, xs))
        )
    ]
    for copy in table_copies:
        copy.start()

    barrier = pltpu.get_barrier_semaphore()

    @pl.loop(0, W)
    def _(k):
        pl.semaphore_signal(barrier, inc=1, device_id=(wide_peer(k), across), device_id_type=MESH)

    for k in (1, 2, 3, 5, 6, 7):
        pl.semaphore_signal(barrier, inc=1, device_id=(w, narrow_peer(k)), device_id_type=MESH)

    odd = parity == 1

    @pl.loop(0, XL)
    def _(a):
        vx, vy, vz, b = vx_ref[a], vy_ref[a], vz_ref[a], b_ref[a]
        data = jnp.concatenate(
            [jnp.where(odd, vy, vx), jnp.where(odd, vx, vy), jnp.where(odd, b, vz), jnp.where(odd, vz, b)], axis=0
        )
        high, low = halves(data)
        nt = ((1,), (1,))
        value = dot(zf[0], high, nt) + dot(zf[1], high, nt) + dot(zf[0], low, nt)
        for g in range(2):
            send1[g, pl.ds(a, MZ, stride=XL), :] = value[:, g * 128 : (g + 1) * 128]

    pl.semaphore_wait(barrier, W + 6)

    def wide_send(src, dst, chunk, ssem, rsem):
        @pl.loop(0, W)
        def _(k):
            peer = wide_peer(k)
            pltpu.make_async_remote_copy(
                src_ref=src.at[:, rows((chunk * W + peer) * XL, XL), :],
                dst_ref=dst.at[:, rows((chunk * W + w) * XL, XL), :],
                send_sem=ssem.at[chunk],
                recv_sem=rsem.at[chunk],
                device_id=(peer, across),
                device_id_type=MESH,
            ).start()

    def narrow_send(src, dst, chunk, ssem, rsem, source_slot, target_slot):
        @pl.loop(1, N)
        def _(k):
            peer = narrow_peer(k)
            pltpu.make_async_remote_copy(
                src_ref=src.at[:, rows((chunk * N + source_slot(peer)) * PL, PL), :],
                dst_ref=dst.at[:, rows((chunk * N + target_slot) * PL, PL), :],
                send_sem=ssem.at[chunk],
                recv_sem=rsem.at[chunk],
                device_id=(w, peer),
                device_id_type=MESH,
            ).start()

        pltpu.make_async_copy(
            src.at[:, rows((chunk * N + source_slot(n)) * PL, PL), :],
            dst.at[:, rows((chunk * N + target_slot) * PL, PL), :],
            rsem.at[chunk],
        ).start()

    def wait(buffer, chunk, size, sem, part=None):
        ref = buffer.at[:, rows(chunk * size, part or size), :]
        pltpu.make_async_copy(ref, ref, sem.at[chunk]).wait()

    @pl.loop(0, QL)
    def _(chunk):
        wide_send(send1, recv1, chunk, s1, r1)

    low_lanes = lax.broadcasted_iota(jnp.int32, (PL, 128), 1) < 64

    def x_step(chunk):
        wait(recv1, chunk, NX, r1)
        for g in range(2):
            high, low = halves(recv1[g, rows(chunk * NX, NX), :])
            xh[:, g * 128 : (g + 1) * 128] = high
            xl[:, g * 128 : (g + 1) * 128] = low

        @pl.loop(0, MX // 256)
        def _(m):
            part = rows(m * 256, 256)
            value = dot3(xf[0, part, :], xf[1, part, :], xh[...], xl[...])
            for g in range(2):
                send2[g, rows(chunk * MX + m * 256, 256), :] = value[:, g * 128 : (g + 1) * 128]

        narrow_send(send2, recv2, chunk, s2, r2, lambda peer: peer, across)

    def y_step(t):
        for q in range(2):
            chunk = 2 * t + q
            wait(recv2, chunk, MX, r2)
            for g in range(2):
                for s in range(4):
                    first = recv2[g, rows(chunk * MX + 2 * s * PL, PL), :]
                    second = recv2[g, rows(chunk * MX + (2 * s + 1) * PL, PL), :]
                    even = jnp.where(low_lanes, first, second)
                    other = pltpu.roll(jnp.where(low_lanes, second, first), 64, 1)
                    for f, value in ((2 * g, even), (2 * g + 1, other)):
                        high, low = halves(value)
                        place = pl.ds((q * 4 + f) * PL, PL)
                        yh[place, s * 128 : (s + 1) * 128] = high
                        yl[place, s * 128 : (s + 1) * 128] = low
        for q in range(2):
            part = pl.ds(q * 4 * PL, 4 * PL)
            for j in range(MY // 256):
                cols = pl.ds(j * 256, 256)
                grid = dot3(yh[part, :], yl[part, :], yf[0, :, cols], yf[1, :, cols])
                for f, place in ((0, 0), (2, 1), (1, 2)):
                    flux = grid[f * PL : (f + 1) * PL] * grid[3 * PL :]
                    high, low = halves(flux)
                    gh[pl.ds((place * 2 + q) * PL, PL), cols] = high
                    gl[pl.ds((place * 2 + q) * PL, PL), cols] = low
        for table, start, fields in ((yb, 0, (0, 2)), (ys, 4 * PL, (1,))):
            part = pl.ds(start, 2 * PL * len(fields))
            for j in range(NY // 256):
                cols = pl.ds(j * 256, 256)
                value = dot3(gh[part, :], gl[part, :], table[0, :, cols], table[1, :, cols])
                for i, f in enumerate(fields):
                    for h in range(2):
                        lanes = slice(h * 128, (h + 1) * 128)
                        first = value[2 * i * PL : (2 * i + 1) * PL, lanes]
                        second = pltpu.roll(value[(2 * i + 1) * PL : (2 * i + 2) * PL, lanes], 64, 1)
                        block = (2 * j + h) * 2
                        send3[f, rows((t * N + block) * PL, PL), :] = jnp.where(low_lanes, first, second)
                        send3[f, rows((t * N + block + 1) * PL, PL), :] = jnp.where(low_lanes, second, first)
        narrow_send(send3, recv3, t, s3, r3, lambda peer: lax.rem(peer + 4, N), n)

    def x_back_step(t):
        wait(recv3, t, MX, r3)
        for f in range(3):
            high, low = halves(recv3[f, rows(t * MX, MX), :])
            bh[:, f * 128 : (f + 1) * 128] = high
            bl[:, f * 128 : (f + 1) * 128] = low

        @pl.loop(0, NX // 256)
        def _(m):
            part = rows(m * 256, 256)
            plain = dot3(xb[0, part, :], xb[1, part, :], bh[:, 128:], bl[:, 128:])
            sloped = dot3(xs[0, part, :], xs[1, part, :], bh[:, :128], bl[:, :128])
            send4[0, rows(t * NX + m * 256, 256), :] = plain[:, :128] + sloped
            send4[1, rows(t * NX + m * 256, 256), :] = plain[:, 128:]

        wide_send(send4, recv4, t, s4, r4)

    for copy in table_copies:
        copy.wait()

    @pl.loop(0, QL + 3)
    def _(i):
        pl.when(i < QL)(lambda: x_step(i))
        even = lax.rem(i, 2) == 0
        pl.when(even & (i >= 4))(lambda: x_back_step(i // 2 - 2))
        pl.when(even & (i >= 2) & (i < QL + 2))(lambda: y_step(i // 2 - 1))

    zh[...] = jnp.zeros_like(zh)
    zl[...] = jnp.zeros_like(zl)
    for t in range(PAIRS):
        wait(recv4, t, NX, r4)
    wide_lanes = lax.broadcasted_iota(jnp.int32, (NZ, 128), 1) < 64

    @pl.loop(0, XL // 2)
    def _(i):
        for side in range(2):
            for g in range(2):
                high, low = halves(recv4[g, pl.ds(2 * i + side, PAIRS * W, stride=XL), :])
                place = pl.ds(g * PAIRS * W, PAIRS * W)
                zh[place, side * 128 : (side + 1) * 128] = high
                zl[place, side * 128 : (side + 1) * 128] = low
        value = dot3(zb[0, parity], zb[1, parity], zh[...], zl[...])
        first = value[:NZ, :128] + pltpu.roll(value[NZ:, :128], 64, 1)
        second = pltpu.roll(value[:NZ, 128:], 64, 1) + value[NZ:, 128:]
        nonlinear = jnp.where(wide_lanes, first, second).T
        for side in range(2):
            buoyancy = b_ref[2 * i + side]
            right_side = buoyancy - (4.0 / NX) * nonlinear[side * YL : (side + 1) * YL]
            out_ref[2 * i + side] = right_side.astype(BF16)

    for c in range(QL):
        wait(send1, c, NX, s1)
        wait(send2, c, MX, s2, MX - PL)
    for t in range(PAIRS):
        wait(send3, t, MX, s3, MX - PL)
        wait(send4, t, NX, s4)


def right_side_of(buoyancy, velocity_x, velocity_y, velocity_z):
    zf, xf, yf, yb, ys, xb, xs, zb = [jnp.asarray(t) for t in tables()]
    vmem = pl.BlockSpec(memory_space=pltpu.VMEM)
    hbm = pl.BlockSpec(memory_space=pl.ANY)
    buffers = []
    for groups, count in ((2, QL * NX), (2, QL * MX), (3, PAIRS * MX), (2, PAIRS * NX)):
        buffers += [pltpu.VMEM((groups, count, 128), F32)] * 2
    split = []
    for shape in ((NX, 256), (8 * PL, NY), (6 * PL, MY), (MX, 384), (256, 256)):
        split += [pltpu.VMEM(shape, BF16)] * 2
    sems = [pltpu.SemaphoreType.DMA((count,)) for count in (6, QL, QL, QL, QL, PAIRS, PAIRS, PAIRS, PAIRS)]
    return pl.pallas_call(
        kernel,
        out_shape=jax.ShapeDtypeStruct((XL, YL, NZ), BF16),
        in_specs=[vmem] * 6 + [hbm] * 6,
        out_specs=vmem,
        scratch_shapes=buffers + [pltpu.VMEM(t.shape, BF16) for t in (xf, yf, yb, ys, xb, xs)] + split + sems,
        compiler_params=pltpu.CompilerParams(
            collective_id=1, has_side_effects=True, vmem_limit_bytes=60 * 1024 * 1024
        ),
        name="spectral",
    )(velocity_x, velocity_y, velocity_z, buoyancy, zf, zb, xf, yf, yb, ys, xb, xs)


def per_device(buoyancy, velocity_x, velocity_y, velocity_z, inverse_blocks):
    right_side = right_side_of(buoyancy, velocity_x, velocity_y, velocity_z)
    grouped = right_side.reshape(XL // 2, 2, YL // 2, 2, NZ)
    solved = jnp.einsum(
        "xyin,xaybn->xaybi", inverse_blocks, grouped, preferred_element_type=F32
    )
    return solved.reshape(XL, YL, NZ)


def solution(mesh):
    fields = P("wide", "narrow", None)
    return jax.shard_map(
        per_device,
        mesh=mesh,
        in_specs=(fields, fields, fields, fields, P("wide", "narrow", None, None)),
        out_specs=fields,
        check_vma=False,
    )
```

```python
import functools

import jax
import jax.numpy as jnp
import ml_dtypes
import numpy as np
from jax import lax
from jax.experimental import pallas as pl
from jax.experimental.pallas import tpu as pltpu
from jax.sharding import PartitionSpec as P

NX = 512
NY = 512
NZ = 128
MX = 768
MY = 768
MZ = 192
W = 32
N = 8
XL = NX // W
YL = NY // N
QL = MZ // W
PL = MX // N
HALF = PL // 2
F32 = jnp.float32
BF16 = jnp.bfloat16
MESH = pl.DeviceIdType.MESH


def fourier_table(n_coef, n_grid):
    index = np.arange(n_coef)
    phase = (index[:, None] // 2 * np.arange(n_grid)[None, :] % n_grid) * (2.0 * np.pi / n_grid)
    return np.where((index % 2 == 0)[:, None], np.cos(phase), np.sin(phase))


def fourier_inverse(n_coef, n_grid):
    index = np.arange(n_coef)
    modes = index // 2
    weight = np.where(modes == 0, np.where(index % 2 == 0, 1.0 / n_grid, 0.0), 2.0 / n_grid)
    return fourier_table(n_coef, n_grid).T * weight[None, :]


def cheb_table(n_coef, n_grid):
    orders = np.arange(n_coef)
    points = np.arange(n_grid)
    index_grid = orders[:, None] * (2 * points[None, :] + 1) % (4 * n_grid)
    return np.cos(index_grid * (np.pi / (2 * n_grid)))


def cheb_inverse(n_coef, n_grid):
    weight = np.where(np.arange(n_coef) == 0, 1.0 / n_grid, 2.0 / n_grid)
    return cheb_table(n_coef, n_grid).T * weight[None, :]


def cheb_slope(n_coef):
    rows = np.arange(n_coef)[:, None]
    cols = np.arange(n_coef)[None, :]
    inside = (cols > rows) & ((cols - rows) % 2 == 1)
    return np.where(inside, np.where(rows == 0, 1.0, 2.0) * cols, 0.0)


def split_table(table):
    high = table.astype(np.float32).astype(ml_dtypes.bfloat16)
    low = (table - high.astype(np.float64)).astype(np.float32).astype(ml_dtypes.bfloat16)
    return np.stack([high, low])


@functools.cache
def tables():
    z_forward = cheb_table(NZ, MZ).T.reshape(W, QL, NZ).transpose(1, 0, 2).reshape(MZ, NZ)
    x_forward = fourier_table(NX, MX).T
    y_forward = fourier_table(NY, MY)
    y_backward = fourier_inverse(NY, MY)
    x_backward = fourier_inverse(NX, MX).T
    plain = cheb_inverse(NZ, MZ)
    z_backward = np.zeros((2, NZ, 256))
    for i, source in enumerate((plain, plain @ cheb_slope(NZ).T)):
        z_backward[i, :, :MZ] = source.reshape(W, QL, NZ).transpose(2, 1, 0).reshape(NZ, MZ)
    z_backward = z_backward.reshape(2 * NZ, 256)
    return [split_table(t) for t in (z_forward, x_forward, y_forward, y_backward, x_backward, z_backward)]


def halves(value):
    high = value.astype(BF16)
    return high, (value - high.astype(F32)).astype(BF16)


def dot(a, b, dims=((1,), (0,))):
    return lax.dot_general(a, b, (dims, ((), ())), preferred_element_type=F32)


def dot3(a_high, a_low, b_high, b_low):
    return dot(a_high, b_high) + dot(a_low, b_high) + dot(a_high, b_low)


def rows(start, size):
    return pl.ds(pl.multiple_of(start, 16), size)


def kernel(
    vx_ref, vy_ref, vz_ref, b_ref, zf, zb, xf_hbm, yf_hbm, yb_hbm, xb_hbm,
    out_ref,
    send1, recv1, send2, recv2, send3, recv3, send4, recv4,
    xf, yf, yb, xb,
    xh, xl, yh, yl, gh, gl, bh, bl, zh, zl,
    table_sem, s1, r1, s2, r2, s3, r3, s4, r4,
):
    w = lax.axis_index("wide")
    n = lax.axis_index("narrow")
    across = lax.rem(n + 4, N)
    parity = lax.rem(n, 2)
    z_pos, rest = w // 4, lax.rem(w, 4)
    y_pos, x_pos = n // 4, lax.rem(n, 4)

    def wide_peer(k):
        step, turn = lax.rem(k, 8), k // 8
        hops = step // 2 + 1
        shift = jnp.where(step == 7, 0, jnp.where(lax.rem(step, 2) == 0, hops, 8 - hops))
        return lax.rem(z_pos + shift, 8) * 4 + lax.rem(rest + turn, 4)

    def narrow_peer(k):
        y_shift = jnp.where(k < 3, lax.rem(k, 3) // 2, jnp.where(k == 5, 0, 1))
        x_shift = jnp.where(
            k < 2, 1 + 2 * k, jnp.where(k == 2, 0, jnp.where(k < 5, 2 * k - 5, 2))
        )
        return lax.rem(y_pos + y_shift, 2) * 4 + lax.rem(x_pos + x_shift, 4)

    def flipped(wide):
        return wide + 2 - 4 * lax.rem(wide // 2, 2)

    def flips(wide, chunk):
        return lax.rem(wide + chunk, 2) == 1

    def plane(chunk):
        return jnp.where(flips(w, chunk) & (y_pos == 0), flipped(w), w)

    table_copies = [
        pltpu.make_async_copy(hbm, vmem, table_sem.at[i])
        for i, (hbm, vmem) in enumerate(
            ((xf_hbm, xf), (yf_hbm, yf), (yb_hbm, yb), (xb_hbm, xb))
        )
    ]
    for copy in table_copies:
        copy.start()

    barrier = pltpu.get_barrier_semaphore()

    @pl.loop(0, W)
    def _(k):
        pl.semaphore_signal(barrier, inc=1, device_id=(wide_peer(k), across), device_id_type=MESH)

    for k in (0, 1, 3, 4, 5, 6):
        pl.semaphore_signal(barrier, inc=1, device_id=(w, narrow_peer(k)), device_id_type=MESH)
    for k in (3, 4, 6):
        pl.semaphore_signal(barrier, inc=1, device_id=(flipped(w), narrow_peer(k)), device_id_type=MESH)

    odd = parity == 1

    @pl.loop(0, XL)
    def _(a):
        vx, vy, vz, b = vx_ref[a], vy_ref[a], vz_ref[a], b_ref[a]
        data = jnp.concatenate(
            [jnp.where(odd, vy, vx), jnp.where(odd, vx, vy), jnp.where(odd, b, vz), jnp.where(odd, vz, b)], axis=0
        )
        high, low = halves(data)
        nt = ((1,), (1,))
        value = dot(zf[0], high, nt) + dot(zf[1], high, nt) + dot(zf[0], low, nt)
        for g in range(2):
            send1[g, pl.ds(a, MZ, stride=XL), :] = value[:, g * 128 : (g + 1) * 128]

    pl.semaphore_wait(barrier, W + 9)

    def wide_send(src, dst, chunk, ssem, rsem, target, slot):
        @pl.loop(0, W)
        def _(k):
            peer = wide_peer(k)
            pltpu.make_async_remote_copy(
                src_ref=src.at[:, rows((chunk * W + peer) * XL, XL), :],
                dst_ref=dst.at[:, rows((chunk * W + slot) * XL, XL), :],
                send_sem=ssem.at[chunk],
                recv_sem=rsem.at[chunk],
                device_id=(target(peer), across),
                device_id_type=MESH,
            ).start()

    def narrow_send(src, dst, chunk, size, ssem, rsem, source_slot, target_slot):
        def block(slot):
            return rows((chunk * N + slot) * size, size)

        @pl.loop(0, N - 1)
        def _(k):
            peer = narrow_peer(k)
            wide = jnp.where(flips(w, chunk) & (peer // 4 != y_pos), flipped(w), w)
            pltpu.make_async_remote_copy(
                src_ref=src.at[:, block(source_slot(peer)), :],
                dst_ref=dst.at[:, block(target_slot), :],
                send_sem=ssem.at[chunk],
                recv_sem=rsem.at[chunk],
                device_id=(wide, peer),
                device_id_type=MESH,
            ).start()

        pltpu.make_async_copy(
            src.at[:, block(source_slot(n)), :], dst.at[:, block(target_slot), :], rsem.at[chunk]
        ).start()

    def wait(buffer, chunk, size, sem, part=None):
        ref = buffer.at[:, rows(chunk * size, part or size), :]
        pltpu.make_async_copy(ref, ref, sem.at[chunk]).wait()

    @pl.loop(0, QL)
    def _(chunk):
        def holder(peer):
            return jnp.where(flips(peer, chunk) & (y_pos == 1), flipped(peer), peer)

        wide_send(send1, recv1, chunk, s1, r1, holder, w)

    low_lanes = lax.broadcasted_iota(jnp.int32, (PL, 128), 1) < 64
    half_lanes = lax.broadcasted_iota(jnp.int32, (HALF, 128), 1) < 64

    def x_step(chunk):
        wait(recv1, chunk, NX, r1)
        for g in range(2):
            high, low = halves(recv1[g, rows(chunk * NX, NX), :])
            xh[:, g * 128 : (g + 1) * 128] = high
            xl[:, g * 128 : (g + 1) * 128] = low

        @pl.loop(0, MX // 256)
        def _(m):
            part = rows(m * 256, 256)
            value = dot3(xf[0, part, :], xf[1, part, :], xh[...], xl[...])
            for g in range(2):
                send2[g, rows(chunk * MX + m * 256, 256), :] = value[:, g * 128 : (g + 1) * 128]

        narrow_send(send2, recv2, chunk, PL, s2, r2, lambda peer: peer, across)

    def y_step(chunk):
        wait(recv2, chunk, MX, r2)
        for g in range(2):
            for s in range(4):
                first = recv2[g, rows(chunk * MX + 2 * s * PL, PL), :]
                second = recv2[g, rows(chunk * MX + (2 * s + 1) * PL, PL), :]
                even = jnp.where(low_lanes, first, second)
                other = pltpu.roll(jnp.where(low_lanes, second, first), 64, 1)
                for f, value in ((2 * g, even), (2 * g + 1, other)):
                    high, low = halves(value)
                    yh[f * PL : (f + 1) * PL, s * 128 : (s + 1) * 128] = high
                    yl[f * PL : (f + 1) * PL, s * 128 : (s + 1) * 128] = low
        for j in range(MY // 256):
            cols = pl.ds(j * 256, 256)
            grid = dot3(yh[...], yl[...], yf[0, :, cols], yf[1, :, cols])
            for f in range(3):
                high, low = halves(grid[f * PL : (f + 1) * PL] * grid[3 * PL :])
                gh[f * PL : (f + 1) * PL, cols] = high
                gl[f * PL : (f + 1) * PL, cols] = low
        lane = lax.broadcasted_iota(jnp.int32, (PL, 128), 1)
        for j in range(NY // 256):
            cols = pl.ds(j * 256, 256)
            value = dot3(gh[...], gl[...], yb[0, :, cols], yb[1, :, cols])
            for f in range(3):
                for h in range(2):
                    part = value[f * PL : (f + 1) * PL, h * 128 : (h + 1) * 128]
                    if f == 1:
                        mode = (lane // 2 + (2 * j + h) * 64).astype(F32)
                        part = jnp.where(
                            lane % 2 == 0, mode * pltpu.roll(part, 127, 1), -mode * pltpu.roll(part, 1, 1)
                        )
                    first, second = part[:HALF], pltpu.roll(part[HALF:], 64, 1)
                    block = chunk * N + (2 * j + h) * 2
                    send3[f, rows(block * HALF, HALF), :] = jnp.where(half_lanes, first, second)
                    send3[f, rows((block + 1) * HALF, HALF), :] = jnp.where(half_lanes, second, first)
        narrow_send(send3, recv3, chunk, HALF, s3, r3, lambda peer: lax.rem(peer + 4, N), n)

    def x_back_step(chunk):
        wait(recv3, chunk, N * HALF, r3)
        for s in range(N):
            flux_x, flux_y, flux_z = (recv3[f, rows((chunk * N + s) * HALF, HALF), :] for f in range(3))
            near = jnp.where(half_lanes, flux_y, pltpu.roll(flux_z, 64, 1))
            far = jnp.where(half_lanes, pltpu.roll(flux_y, 64, 1), flux_z)
            for side, yz, x in ((parity, near, flux_x), (1 - parity, far, pltpu.roll(flux_x, 64, 1))):
                place = rows(s * PL + side * HALF, HALF)
                for lanes, value in ((slice(0, 128), yz), (slice(128, 256), x)):
                    high, low = halves(value)
                    bh[place, lanes] = high
                    bl[place, lanes] = low

        row = lax.broadcasted_iota(jnp.int32, (256, 128), 0)
        lane = lax.broadcasted_iota(jnp.int32, (256, 128), 1)
        for m in range(NX // 256):
            part = pl.ds(m * 256, 256)
            value = dot3(xb[0, part, :], xb[1, part, :], bh[...], bl[...])
            x = value[:, 128:]
            mode = (row // 2 + m * 128).astype(F32)
            sloped = jnp.where(row % 2 == 0, mode * pltpu.roll(x, 255, 0), -mode * pltpu.roll(x, 1, 0))
            send4[0, rows(chunk * NX + m * 256, 256), :] = value[:, :128] + jnp.where(lane < 64, sloped, 0.0)

        wide_send(send4, recv4, chunk, s4, r4, lambda peer: peer, plane(chunk))

    for copy in table_copies:
        copy.wait()

    @pl.loop(0, QL + 2)
    def _(i):
        pl.when(i < QL)(lambda: x_step(i))
        pl.when((i >= 1) & (i < QL + 1))(lambda: y_step(i - 1))
        pl.when(i >= 2)(lambda: x_back_step(i - 2))

    zh[...] = jnp.zeros_like(zh)
    zl[...] = jnp.zeros_like(zl)
    for c in range(QL):
        wait(recv4, c, NX, r4)
    wide_lanes = lax.broadcasted_iota(jnp.int32, (NZ, 128), 1) < 64

    @pl.loop(0, XL // 2)
    def _(i):
        for side in range(2):
            high, low = halves(recv4[0, pl.ds(2 * i + side, MZ, stride=XL), :])
            zh[:MZ, side * 128 : (side + 1) * 128] = high
            zl[:MZ, side * 128 : (side + 1) * 128] = low
        value = dot3(zb[0], zb[1], zh[...], zl[...])
        first = value[:NZ, :128] + pltpu.roll(value[NZ:, :128], 64, 1)
        second = pltpu.roll(value[:NZ, 128:], 64, 1) + value[NZ:, 128:]
        nonlinear = jnp.where(wide_lanes, first, second).T
        for side in range(2):
            buoyancy = b_ref[2 * i + side]
            right_side = buoyancy - (4.0 / NX) * nonlinear[side * YL : (side + 1) * YL]
            out_ref[2 * i + side] = right_side.astype(BF16)

    for c in range(QL):
        wait(send1, c, NX, s1)
        wait(send2, c, MX, s2, MX - PL)
        wait(send3, c, N * HALF, s3, (N - 1) * HALF)
        wait(send4, c, NX, s4)


def right_side_of(buoyancy, velocity_x, velocity_y, velocity_z):
    zf, xf, yf, yb, xb, zb = [jnp.asarray(t) for t in tables()]
    vmem = pl.BlockSpec(memory_space=pltpu.VMEM)
    hbm = pl.BlockSpec(memory_space=pl.ANY)
    buffers = []
    for groups, count in ((2, QL * NX), (2, QL * MX), (3, QL * N * HALF), (1, QL * NX)):
        buffers += [pltpu.VMEM((groups, count, 128), F32)] * 2
    split = []
    for shape in ((NX, 256), (4 * PL, NY), (3 * PL, MY), (MX, 256), (256, 256)):
        split += [pltpu.VMEM(shape, BF16)] * 2
    sems = [pltpu.SemaphoreType.DMA((count,)) for count in (4,) + (QL,) * 8]
    return pl.pallas_call(
        kernel,
        out_shape=jax.ShapeDtypeStruct((XL, YL, NZ), BF16),
        in_specs=[vmem] * 6 + [hbm] * 4,
        out_specs=vmem,
        scratch_shapes=buffers + [pltpu.VMEM(t.shape, BF16) for t in (xf, yf, yb, xb)] + split + sems,
        compiler_params=pltpu.CompilerParams(
            collective_id=1, has_side_effects=True, vmem_limit_bytes=60 * 1024 * 1024
        ),
        name="spectral",
    )(velocity_x, velocity_y, velocity_z, buoyancy, zf, zb, xf, yf, yb, xb)


def per_device(buoyancy, velocity_x, velocity_y, velocity_z, inverse_blocks):
    right_side = right_side_of(buoyancy, velocity_x, velocity_y, velocity_z)
    grouped = right_side.reshape(XL // 2, 2, YL // 2, 2, NZ)
    solved = jnp.einsum(
        "xyin,xaybn->xaybi", inverse_blocks, grouped, preferred_element_type=F32
    )
    return solved.reshape(XL, YL, NZ)


def solution(mesh):
    fields = P("wide", "narrow", None)
    return jax.shard_map(
        per_device,
        mesh=mesh,
        in_specs=(fields, fields, fields, fields, P("wide", "narrow", None, None)),
        out_specs=fields,
        check_vma=False,
    )
```

```python
import functools

import jax
import jax.numpy as jnp
import ml_dtypes
import numpy as np
from jax import lax
from jax.experimental import pallas as pl
from jax.experimental.pallas import tpu as pltpu
from jax.sharding import PartitionSpec as P

NX = 512
NY = 512
NZ = 128
MX = 768
MY = 768
MZ = 192
W = 32
N = 8
XL = NX // W
YL = NY // N
QL = MZ // W
PL = MX // N
HALF = PL // 2
F32 = jnp.float32
BF16 = jnp.bfloat16
MESH = pl.DeviceIdType.MESH


def fourier_table(n_coef, n_grid):
    index = np.arange(n_coef)
    phase = (index[:, None] // 2 * np.arange(n_grid)[None, :] % n_grid) * (2.0 * np.pi / n_grid)
    return np.where((index % 2 == 0)[:, None], np.cos(phase), np.sin(phase))


def fourier_inverse(n_coef, n_grid):
    index = np.arange(n_coef)
    modes = index // 2
    weight = np.where(modes == 0, np.where(index % 2 == 0, 1.0 / n_grid, 0.0), 2.0 / n_grid)
    return fourier_table(n_coef, n_grid).T * weight[None, :]


def cheb_table(n_coef, n_grid):
    orders = np.arange(n_coef)
    points = np.arange(n_grid)
    index_grid = orders[:, None] * (2 * points[None, :] + 1) % (4 * n_grid)
    return np.cos(index_grid * (np.pi / (2 * n_grid)))


def cheb_inverse(n_coef, n_grid):
    weight = np.where(np.arange(n_coef) == 0, 1.0 / n_grid, 2.0 / n_grid)
    return cheb_table(n_coef, n_grid).T * weight[None, :]


def cheb_slope(n_coef):
    rows = np.arange(n_coef)[:, None]
    cols = np.arange(n_coef)[None, :]
    inside = (cols > rows) & ((cols - rows) % 2 == 1)
    return np.where(inside, np.where(rows == 0, 1.0, 2.0) * cols, 0.0)


def split_table(table):
    high = table.astype(np.float32).astype(ml_dtypes.bfloat16)
    low = (table - high.astype(np.float64)).astype(np.float32).astype(ml_dtypes.bfloat16)
    return np.stack([high, low])


@functools.cache
def tables():
    z_forward = cheb_table(NZ, MZ).T.reshape(W, QL, NZ).transpose(1, 0, 2).reshape(MZ, NZ)
    x_forward = fourier_table(NX, MX).T
    y_forward = fourier_table(NY, MY)
    y_backward = fourier_inverse(NY, MY)
    x_backward = fourier_inverse(NX, MX).T
    plain = cheb_inverse(NZ, MZ)
    z_backward = np.zeros((2, NZ, 256))
    for i, source in enumerate((plain, plain @ cheb_slope(NZ).T)):
        z_backward[i, :, :MZ] = source.reshape(W, QL, NZ).transpose(2, 1, 0).reshape(NZ, MZ)
    z_backward = z_backward.reshape(2 * NZ, 256)
    return [split_table(t) for t in (z_forward, x_forward, y_forward, y_backward, x_backward, z_backward)]


def halves(value):
    high = value.astype(BF16)
    return high, (value - high.astype(F32)).astype(BF16)


def dot(a, b, dims=((1,), (0,))):
    return lax.dot_general(a, b, (dims, ((), ())), preferred_element_type=F32)


def dot3(a_high, a_low, b_high, b_low):
    return dot(a_high, b_high) + dot(a_low, b_high) + dot(a_high, b_low)


def rows(start, size):
    return pl.ds(pl.multiple_of(start, 16), size)


def kernel(
    vx_hbm, vy_hbm, vz_hbm, b_hbm, zf_hbm, zb_hbm, xf_hbm, yf_hbm, yb_hbm, xb_hbm,
    out_ref,
    send1, recv1, send2, recv2, send3, recv3, send4, recv4,
    vx_ref, vy_ref, vz_ref, b_ref, zf, zb, xf, yf, yb, xb,
    xh, xl, yh, yl, gh, gl, bh, bl, zh, zl,
    table_sem, s1, r1, s2, r2, s3, r3, s4, r4,
):
    w = lax.axis_index("wide")
    n = lax.axis_index("narrow")
    across = lax.rem(n + 4, N)
    parity = lax.rem(n, 2)
    z_pos, rest = w // 4, lax.rem(w, 4)
    y_pos, x_pos = n // 4, lax.rem(n, 4)

    def wide_peer(k):
        step, turn = lax.rem(k, 8), k // 8
        hops = step // 2 + 1
        shift = jnp.where(step == 7, 0, jnp.where(lax.rem(step, 2) == 0, hops, 8 - hops))
        return lax.rem(z_pos + shift, 8) * 4 + lax.rem(rest + turn, 4)

    def narrow_peer(k):
        y_shift = jnp.where(k < 3, lax.rem(k, 3) // 2, jnp.where(k == 5, 0, 1))
        x_shift = jnp.where(
            k < 2, 1 + 2 * k, jnp.where(k == 2, 0, jnp.where(k < 5, 2 * k - 5, 2))
        )
        return lax.rem(y_pos + y_shift, 2) * 4 + lax.rem(x_pos + x_shift, 4)

    def flipped(wide):
        return wide + 2 - 4 * lax.rem(wide // 2, 2)

    def flips(wide, chunk):
        return lax.rem(wide + chunk, 2) == 1

    def plane(chunk):
        return jnp.where(flips(w, chunk) & (y_pos == 0), flipped(w), w)

    table_copies = [
        pltpu.make_async_copy(hbm, vmem, table_sem.at[i])
        for i, (hbm, vmem) in enumerate(
            (
                (vx_hbm, vx_ref), (vy_hbm, vy_ref), (vz_hbm, vz_ref), (b_hbm, b_ref), (zf_hbm, zf),
                (xf_hbm, xf), (yf_hbm, yf), (yb_hbm, yb), (xb_hbm, xb), (zb_hbm, zb),
            )
        )
    ]
    for copy in table_copies:
        copy.start()

    barrier = pltpu.get_barrier_semaphore()

    @pl.loop(0, W)
    def _(k):
        pl.semaphore_signal(barrier, inc=1, device_id=(wide_peer(k), across), device_id_type=MESH)

    for k in (0, 1, 3, 4, 5, 6):
        pl.semaphore_signal(barrier, inc=1, device_id=(w, narrow_peer(k)), device_id_type=MESH)
    for k in (3, 4, 6):
        pl.semaphore_signal(barrier, inc=1, device_id=(flipped(w), narrow_peer(k)), device_id_type=MESH)

    for copy in table_copies[:5]:
        copy.wait()
    odd = parity == 1

    def z_step(a, part, size):
        vx, vy, vz, b = vx_ref[a], vy_ref[a], vz_ref[a], b_ref[a]
        data = jnp.concatenate(
            [jnp.where(odd, vy, vx), jnp.where(odd, vx, vy), jnp.where(odd, b, vz), jnp.where(odd, vz, b)], axis=0
        )
        high, low = halves(data)
        nt = ((1,), (1,))
        first, second = zf[0, part : part + size], zf[1, part : part + size]
        value = dot(first, high, nt) + dot(second, high, nt) + dot(first, low, nt)
        for g in range(2):
            send1[g, pl.ds(part * XL + a, size, stride=XL), :] = value[:, g * 128 : (g + 1) * 128]

    @pl.loop(0, XL)
    def _(a):
        z_step(a, 0, W)

    pl.semaphore_wait(barrier, W + 9)

    def wide_send(src, dst, chunk, ssem, rsem, target, slot):
        @pl.loop(0, W)
        def _(k):
            peer = wide_peer(k)
            pltpu.make_async_remote_copy(
                src_ref=src.at[:, rows((chunk * W + peer) * XL, XL), :],
                dst_ref=dst.at[:, rows((chunk * W + slot) * XL, XL), :],
                send_sem=ssem.at[chunk],
                recv_sem=rsem.at[chunk],
                device_id=(target(peer), across),
                device_id_type=MESH,
            ).start()

    def narrow_send(src, dst, chunk, size, ssem, rsem, source_slot, target_slot):
        def block(slot):
            return rows((chunk * N + slot) * size, size)

        @pl.loop(0, N - 1)
        def _(k):
            peer = narrow_peer(k)
            wide = jnp.where(flips(w, chunk) & (peer // 4 != y_pos), flipped(w), w)
            pltpu.make_async_remote_copy(
                src_ref=src.at[:, block(source_slot(peer)), :],
                dst_ref=dst.at[:, block(target_slot), :],
                send_sem=ssem.at[chunk],
                recv_sem=rsem.at[chunk],
                device_id=(wide, peer),
                device_id_type=MESH,
            ).start()

        pltpu.make_async_copy(
            src.at[:, block(source_slot(n)), :], dst.at[:, block(target_slot), :], rsem.at[chunk]
        ).start()

    def wait(buffer, chunk, size, sem, part=None):
        ref = buffer.at[:, rows(chunk * size, part or size), :]
        pltpu.make_async_copy(ref, ref, sem.at[chunk]).wait()

    def forward(chunk):
        def holder(peer):
            return jnp.where(flips(peer, chunk) & (y_pos == 1), flipped(peer), peer)

        wide_send(send1, recv1, chunk, s1, r1, holder, w)

    forward(0)

    @pl.loop(0, XL)
    def _(a):
        z_step(a, W, MZ - W)

    @pl.loop(1, QL)
    def _(chunk):
        forward(chunk)

    low_lanes = lax.broadcasted_iota(jnp.int32, (PL, 128), 1) < 64
    half_lanes = lax.broadcasted_iota(jnp.int32, (HALF, 128), 1) < 64

    def x_step(chunk):
        wait(recv1, chunk, NX, r1)
        for g in range(2):
            high, low = halves(recv1[g, rows(chunk * NX, NX), :])
            xh[:, g * 128 : (g + 1) * 128] = high
            xl[:, g * 128 : (g + 1) * 128] = low

        @pl.loop(0, MX // 256)
        def _(m):
            part = rows(m * 256, 256)
            value = dot3(xf[0, part, :], xf[1, part, :], xh[...], xl[...])
            for g in range(2):
                send2[g, rows(chunk * MX + m * 256, 256), :] = value[:, g * 128 : (g + 1) * 128]

        narrow_send(send2, recv2, chunk, PL, s2, r2, lambda peer: peer, across)

    def y_step(chunk):
        wait(recv2, chunk, MX, r2)
        for g in range(2):
            for s in range(4):
                first = recv2[g, rows(chunk * MX + 2 * s * PL, PL), :]
                second = recv2[g, rows(chunk * MX + (2 * s + 1) * PL, PL), :]
                even = jnp.where(low_lanes, first, second)
                other = pltpu.roll(jnp.where(low_lanes, second, first), 64, 1)
                for f, value in ((2 * g, even), (2 * g + 1, other)):
                    high, low = halves(value)
                    yh[f * PL : (f + 1) * PL, s * 128 : (s + 1) * 128] = high
                    yl[f * PL : (f + 1) * PL, s * 128 : (s + 1) * 128] = low
        for j in range(MY // 256):
            cols = pl.ds(j * 256, 256)
            grid = dot3(yh[...], yl[...], yf[0, :, cols], yf[1, :, cols])
            for f in range(3):
                high, low = halves(grid[f * PL : (f + 1) * PL] * grid[3 * PL :])
                gh[f * PL : (f + 1) * PL, cols] = high
                gl[f * PL : (f + 1) * PL, cols] = low
        lane = lax.broadcasted_iota(jnp.int32, (PL, 128), 1)
        for j in range(NY // 256):
            cols = pl.ds(j * 256, 256)
            value = dot3(gh[...], gl[...], yb[0, :, cols], yb[1, :, cols])
            for f in range(3):
                for h in range(2):
                    part = value[f * PL : (f + 1) * PL, h * 128 : (h + 1) * 128]
                    if f == 1:
                        mode = (lane // 2 + (2 * j + h) * 64).astype(F32)
                        part = jnp.where(
                            lane % 2 == 0, mode * pltpu.roll(part, 127, 1), -mode * pltpu.roll(part, 1, 1)
                        )
                    first, second = part[:HALF], pltpu.roll(part[HALF:], 64, 1)
                    block = chunk * N + (2 * j + h) * 2
                    send3[f, rows(block * HALF, HALF), :] = jnp.where(half_lanes, first, second)
                    send3[f, rows((block + 1) * HALF, HALF), :] = jnp.where(half_lanes, second, first)
        narrow_send(send3, recv3, chunk, HALF, s3, r3, lambda peer: lax.rem(peer + 4, N), n)

    def x_back_step(chunk):
        wait(recv3, chunk, N * HALF, r3)
        for s in range(N):
            flux_x, flux_y, flux_z = (recv3[f, rows((chunk * N + s) * HALF, HALF), :] for f in range(3))
            near = jnp.where(half_lanes, flux_y, pltpu.roll(flux_z, 64, 1))
            far = jnp.where(half_lanes, pltpu.roll(flux_y, 64, 1), flux_z)
            for side, yz, x in ((parity, near, flux_x), (1 - parity, far, pltpu.roll(flux_x, 64, 1))):
                place = rows(s * PL + side * HALF, HALF)
                for lanes, value in ((slice(0, 128), yz), (slice(128, 256), x)):
                    high, low = halves(value)
                    bh[place, lanes] = high
                    bl[place, lanes] = low

        row = lax.broadcasted_iota(jnp.int32, (256, 128), 0)
        lane = lax.broadcasted_iota(jnp.int32, (256, 128), 1)
        for m in range(NX // 256):
            part = pl.ds(m * 256, 256)
            value = dot3(xb[0, part, :], xb[1, part, :], bh[...], bl[...])
            x = value[:, 128:]
            mode = (row // 2 + m * 128).astype(F32)
            sloped = jnp.where(row % 2 == 0, mode * pltpu.roll(x, 255, 0), -mode * pltpu.roll(x, 1, 0))
            send4[0, rows(chunk * NX + m * 256, 256), :] = value[:, :128] + jnp.where(lane < 64, sloped, 0.0)

        wide_send(send4, recv4, chunk, s4, r4, lambda peer: peer, plane(chunk))

    for copy in table_copies[5:]:
        copy.wait()

    @pl.loop(0, QL + 2)
    def _(i):
        pl.when(i < QL)(lambda: x_step(i))
        pl.when((i >= 1) & (i < QL + 1))(lambda: y_step(i - 1))
        pl.when(i >= 2)(lambda: x_back_step(i - 2))

    zh[...] = jnp.zeros_like(zh)
    zl[...] = jnp.zeros_like(zl)
    for c in range(QL):
        wait(recv4, c, NX, r4)
    wide_lanes = lax.broadcasted_iota(jnp.int32, (NZ, 128), 1) < 64

    @pl.loop(0, XL // 2)
    def _(i):
        for side in range(2):
            high, low = halves(recv4[0, pl.ds(2 * i + side, MZ, stride=XL), :])
            zh[:MZ, side * 128 : (side + 1) * 128] = high
            zl[:MZ, side * 128 : (side + 1) * 128] = low
        value = dot3(zb[0], zb[1], zh[...], zl[...])
        first = value[:NZ, :128] + pltpu.roll(value[NZ:, :128], 64, 1)
        second = pltpu.roll(value[:NZ, 128:], 64, 1) + value[NZ:, 128:]
        nonlinear = jnp.where(wide_lanes, first, second).T
        for side in range(2):
            buoyancy = b_ref[2 * i + side]
            right_side = buoyancy - (4.0 / NX) * nonlinear[side * YL : (side + 1) * YL]
            out_ref[2 * i + side] = right_side.astype(BF16)

    for c in range(QL):
        wait(send1, c, NX, s1)
        wait(send2, c, MX, s2, MX - PL)
        wait(send3, c, N * HALF, s3, (N - 1) * HALF)
        wait(send4, c, NX, s4)


def right_side_of(buoyancy, velocity_x, velocity_y, velocity_z):
    zf, xf, yf, yb, xb, zb = [jnp.asarray(t) for t in tables()]
    vmem = pl.BlockSpec(memory_space=pltpu.VMEM)
    hbm = pl.BlockSpec(memory_space=pltpu.HBM)
    fields = [pltpu.VMEM((XL, YL, NZ), F32)] * 4
    buffers = []
    for groups, count in ((2, QL * NX), (2, QL * MX), (3, QL * N * HALF), (1, QL * NX)):
        buffers += [pltpu.VMEM((groups, count, 128), F32)] * 2
    split = []
    for shape in ((NX, 256), (4 * PL, NY), (3 * PL, MY), (MX, 256), (256, 256)):
        split += [pltpu.VMEM(shape, BF16)] * 2
    sems = [pltpu.SemaphoreType.DMA((count,)) for count in (10,) + (QL,) * 8]
    return pl.pallas_call(
        kernel,
        out_shape=jax.ShapeDtypeStruct((XL, YL, NZ), BF16),
        in_specs=[hbm] * 10,
        out_specs=vmem,
        scratch_shapes=buffers + fields + [pltpu.VMEM(t.shape, BF16) for t in (zf, zb, xf, yf, yb, xb)] + split + sems,
        compiler_params=pltpu.CompilerParams(
            collective_id=1, has_side_effects=True, vmem_limit_bytes=55 * 1024 * 1024
        ),
        name="spectral",
    )(velocity_x, velocity_y, velocity_z, buoyancy, zf, zb, xf, yf, yb, xb)


def per_device(buoyancy, velocity_x, velocity_y, velocity_z, inverse_blocks):
    right_side = right_side_of(buoyancy, velocity_x, velocity_y, velocity_z)
    grouped = right_side.reshape(XL // 2, 2, YL // 2, 2, NZ)
    solved = jnp.einsum(
        "xyin,xaybn->xaybi", inverse_blocks, grouped, preferred_element_type=F32
    )
    return solved.reshape(XL, YL, NZ)


def solution(mesh):
    fields = P("wide", "narrow", None)
    return jax.shard_map(
        per_device,
        mesh=mesh,
        in_specs=(fields, fields, fields, fields, P("wide", "narrow", None, None)),
        out_specs=fields,
        check_vma=False,
    )
```

```python
import functools

import jax
import jax.numpy as jnp
import ml_dtypes
import numpy as np
from jax import lax
from jax.experimental import pallas as pl
from jax.experimental.pallas import tpu as pltpu
from jax.sharding import PartitionSpec as P

NX = 512
NY = 512
NZ = 128
MX = 768
MY = 768
MZ = 192
W = 32
N = 8
XL = NX // W
YL = NY // N
QL = MZ // W
PL = MX // N
HALF = PL // 2
F32 = jnp.float32
BF16 = jnp.bfloat16
MESH = pl.DeviceIdType.MESH


def fourier_table(n_coef, n_grid):
    index = np.arange(n_coef)
    phase = (index[:, None] // 2 * np.arange(n_grid)[None, :] % n_grid) * (2.0 * np.pi / n_grid)
    return np.where((index % 2 == 0)[:, None], np.cos(phase), np.sin(phase))


def fourier_inverse(n_coef, n_grid):
    index = np.arange(n_coef)
    modes = index // 2
    weight = np.where(modes == 0, np.where(index % 2 == 0, 1.0 / n_grid, 0.0), 2.0 / n_grid)
    return fourier_table(n_coef, n_grid).T * weight[None, :]


def cheb_table(n_coef, n_grid):
    orders = np.arange(n_coef)
    points = np.arange(n_grid)
    index_grid = orders[:, None] * (2 * points[None, :] + 1) % (4 * n_grid)
    return np.cos(index_grid * (np.pi / (2 * n_grid)))


def cheb_inverse(n_coef, n_grid):
    weight = np.where(np.arange(n_coef) == 0, 1.0 / n_grid, 2.0 / n_grid)
    return cheb_table(n_coef, n_grid).T * weight[None, :]


def cheb_slope(n_coef):
    rows = np.arange(n_coef)[:, None]
    cols = np.arange(n_coef)[None, :]
    inside = (cols > rows) & ((cols - rows) % 2 == 1)
    return np.where(inside, np.where(rows == 0, 1.0, 2.0) * cols, 0.0)


def split_table(table):
    high = table.astype(np.float32).astype(ml_dtypes.bfloat16)
    low = (table - high.astype(np.float64)).astype(np.float32).astype(ml_dtypes.bfloat16)
    return np.stack([high, low])


@functools.cache
def tables():
    z_forward = cheb_table(NZ, MZ).T.reshape(W, QL, NZ).transpose(1, 0, 2).reshape(MZ, NZ)
    x_forward = fourier_table(NX, MX).T
    y_forward = fourier_table(NY, MY)
    y_backward = fourier_inverse(NY, MY)
    x_backward = fourier_inverse(NX, MX).T
    plain = cheb_inverse(NZ, MZ)
    z_backward = np.zeros((2, NZ, 256))
    for i, source in enumerate((plain, plain @ cheb_slope(NZ).T)):
        z_backward[i, :, :MZ] = source.reshape(W, QL, NZ).transpose(2, 1, 0).reshape(NZ, MZ)
    z_backward = z_backward.reshape(2 * NZ, 256)
    return [split_table(t) for t in (z_forward, x_forward, y_forward, y_backward, x_backward, z_backward)]


def halves(value):
    high = value.astype(BF16)
    return high, (value - high.astype(F32)).astype(BF16)


def dot(a, b, dims=((1,), (0,))):
    return lax.dot_general(a, b, (dims, ((), ())), preferred_element_type=F32)


def dot3(a_high, a_low, b_high, b_low):
    return dot(a_high, b_high) + dot(a_low, b_high) + dot(a_high, b_low)


def rows(start, size):
    return pl.ds(pl.multiple_of(start, 16), size)


def kernel(
    vx_hbm, vy_hbm, vz_hbm, b_hbm, zf_hbm, zb_hbm, xf_hbm, yf_hbm, yb_hbm, xb_hbm,
    out_ref,
    send1, recv1, send2, recv2, send3, recv3, send4, recv4,
    vx_ref, vy_ref, vz_ref, b_ref, zf, zb, xf, yf, yb, xb,
    xh, xl, yh, yl, gh, gl, bh, bl, zh, zl,
    table_sem, s1, r1, s2, r2, s3, r3, s4, r4,
):
    w = lax.axis_index("wide")
    n = lax.axis_index("narrow")
    across = lax.rem(n + 4, N)
    parity = lax.rem(n, 2)
    z_pos, rest = w // 4, lax.rem(w, 4)
    y_pos, x_pos = n // 4, lax.rem(n, 4)

    def wide_peer(k):
        step, turn = lax.rem(k, 8), k // 8
        away = (step + 1) // 2
        shift = jnp.where(lax.rem(step, 2) == 1, 4 - away, 4 + away)
        return lax.rem(z_pos + shift, 8) * 4 + lax.rem(rest + turn, 4)

    def narrow_peer(k):
        y_shift = jnp.where((k == 0) | (k == 2) | (k == 3) | (k == 6), 1, 0)
        x_shift = jnp.where(k < 2, 2, jnp.where(k == 6, 0, 1 + 2 * lax.rem(k, 2)))
        return lax.rem(y_pos + y_shift, 2) * 4 + lax.rem(x_pos + x_shift, 4)

    def flipped(wide):
        return wide + 2 - 4 * lax.rem(wide // 2, 2)

    def flips(wide, chunk):
        return lax.rem(wide + chunk, 2) == 1

    def plane(chunk):
        return jnp.where(flips(w, chunk) & (y_pos == 0), flipped(w), w)

    table_copies = [
        pltpu.make_async_copy(hbm, vmem, table_sem.at[i])
        for i, (hbm, vmem) in enumerate(
            (
                (vx_hbm, vx_ref), (vy_hbm, vy_ref), (vz_hbm, vz_ref), (b_hbm, b_ref), (zf_hbm, zf),
                (xf_hbm, xf), (yf_hbm, yf), (yb_hbm, yb), (xb_hbm, xb), (zb_hbm, zb),
            )
        )
    ]
    for copy in table_copies:
        copy.start()

    barrier = pltpu.get_barrier_semaphore()

    @pl.loop(0, W)
    def _(k):
        pl.semaphore_signal(barrier, inc=1, device_id=(wide_peer(k), across), device_id_type=MESH)

    for k in range(6):
        pl.semaphore_signal(barrier, inc=1, device_id=(w, narrow_peer(k)), device_id_type=MESH)
    for k in (0, 2, 3):
        pl.semaphore_signal(barrier, inc=1, device_id=(flipped(w), narrow_peer(k)), device_id_type=MESH)

    for copy in table_copies[:5]:
        copy.wait()
    odd = parity == 1

    def z_step(a, part, size):
        vx, vy, vz, b = vx_ref[a], vy_ref[a], vz_ref[a], b_ref[a]
        data = jnp.concatenate(
            [jnp.where(odd, vy, vx), jnp.where(odd, vx, vy), jnp.where(odd, b, vz), jnp.where(odd, vz, b)], axis=0
        )
        high, low = halves(data)
        nt = ((1,), (1,))
        first, second = zf[0, part : part + size], zf[1, part : part + size]
        value = dot(first, high, nt) + dot(second, high, nt) + dot(first, low, nt)
        for g in range(2):
            send1[g, pl.ds(part * XL + a, size, stride=XL), :] = value[:, g * 128 : (g + 1) * 128]

    @pl.loop(0, XL)
    def _(a):
        z_step(a, 0, W)

    pl.semaphore_wait(barrier, W + 9)

    def wide_send(src, dst, chunk, ssem, rsem, target, slot):
        @pl.loop(0, W)
        def _(k):
            peer = wide_peer(k)
            pltpu.make_async_remote_copy(
                src_ref=src.at[:, rows((chunk * W + peer) * XL, XL), :],
                dst_ref=dst.at[:, rows((chunk * W + slot) * XL, XL), :],
                send_sem=ssem.at[chunk],
                recv_sem=rsem.at[chunk],
                device_id=(target(peer), across),
                device_id_type=MESH,
            ).start()

    def narrow_send(src, dst, chunk, size, ssem, rsem, source_slot, target_slot):
        def block(slot):
            return rows((chunk * N + slot) * size, size)

        @pl.loop(0, N - 1)
        def _(k):
            peer = narrow_peer(k)
            wide = jnp.where(flips(w, chunk) & (peer // 4 != y_pos), flipped(w), w)
            pltpu.make_async_remote_copy(
                src_ref=src.at[:, block(source_slot(peer)), :],
                dst_ref=dst.at[:, block(target_slot), :],
                send_sem=ssem.at[chunk],
                recv_sem=rsem.at[chunk],
                device_id=(wide, peer),
                device_id_type=MESH,
            ).start()

        pltpu.make_async_copy(
            src.at[:, block(source_slot(n)), :], dst.at[:, block(target_slot), :], rsem.at[chunk]
        ).start()

    def wait(buffer, chunk, size, sem, part=None):
        ref = buffer.at[:, rows(chunk * size, part or size), :]
        pltpu.make_async_copy(ref, ref, sem.at[chunk]).wait()

    def forward(chunk):
        def holder(peer):
            return jnp.where(flips(peer, chunk) & (y_pos == 1), flipped(peer), peer)

        wide_send(send1, recv1, chunk, s1, r1, holder, w)

    forward(0)

    @pl.loop(0, XL)
    def _(a):
        z_step(a, W, MZ - W)

    @pl.loop(1, QL)
    def _(chunk):
        forward(chunk)

    low_lanes = lax.broadcasted_iota(jnp.int32, (PL, 128), 1) < 64
    half_lanes = lax.broadcasted_iota(jnp.int32, (HALF, 128), 1) < 64

    def x_step(chunk):
        wait(recv1, chunk, NX, r1)
        for g in range(2):
            high, low = halves(recv1[g, rows(chunk * NX, NX), :])
            xh[:, g * 128 : (g + 1) * 128] = high
            xl[:, g * 128 : (g + 1) * 128] = low

        @pl.loop(0, MX // 256)
        def _(m):
            part = rows(m * 256, 256)
            value = dot3(xf[0, part, :], xf[1, part, :], xh[...], xl[...])
            for g in range(2):
                send2[g, rows(chunk * MX + m * 256, 256), :] = value[:, g * 128 : (g + 1) * 128]

        narrow_send(send2, recv2, chunk, PL, s2, r2, lambda peer: peer, across)

    def y_step(chunk):
        wait(recv2, chunk, MX, r2)
        for g in range(2):
            for s in range(4):
                first = recv2[g, rows(chunk * MX + 2 * s * PL, PL), :]
                second = recv2[g, rows(chunk * MX + (2 * s + 1) * PL, PL), :]
                even = jnp.where(low_lanes, first, second)
                other = pltpu.roll(jnp.where(low_lanes, second, first), 64, 1)
                for f, value in ((2 * g, even), (2 * g + 1, other)):
                    high, low = halves(value)
                    yh[f * PL : (f + 1) * PL, s * 128 : (s + 1) * 128] = high
                    yl[f * PL : (f + 1) * PL, s * 128 : (s + 1) * 128] = low
        for j in range(MY // 256):
            cols = pl.ds(j * 256, 256)
            grid = dot3(yh[...], yl[...], yf[0, :, cols], yf[1, :, cols])
            for f in range(3):
                high, low = halves(grid[f * PL : (f + 1) * PL] * grid[3 * PL :])
                gh[f * PL : (f + 1) * PL, cols] = high
                gl[f * PL : (f + 1) * PL, cols] = low
        lane = lax.broadcasted_iota(jnp.int32, (PL, 128), 1)
        for j in range(NY // 256):
            cols = pl.ds(j * 256, 256)
            value = dot3(gh[...], gl[...], yb[0, :, cols], yb[1, :, cols])
            for f in range(3):
                for h in range(2):
                    part = value[f * PL : (f + 1) * PL, h * 128 : (h + 1) * 128]
                    if f == 1:
                        mode = (lane // 2 + (2 * j + h) * 64).astype(F32)
                        part = jnp.where(
                            lane % 2 == 0, mode * pltpu.roll(part, 127, 1), -mode * pltpu.roll(part, 1, 1)
                        )
                    first, second = part[:HALF], pltpu.roll(part[HALF:], 64, 1)
                    block = chunk * N + (2 * j + h) * 2
                    send3[f, rows(block * HALF, HALF), :] = jnp.where(half_lanes, first, second)
                    send3[f, rows((block + 1) * HALF, HALF), :] = jnp.where(half_lanes, second, first)
        narrow_send(send3, recv3, chunk, HALF, s3, r3, lambda peer: lax.rem(peer + 4, N), n)

    def x_back_step(chunk):
        wait(recv3, chunk, N * HALF, r3)
        for s in range(N):
            flux_x, flux_y, flux_z = (recv3[f, rows((chunk * N + s) * HALF, HALF), :] for f in range(3))
            near = jnp.where(half_lanes, flux_y, pltpu.roll(flux_z, 64, 1))
            far = jnp.where(half_lanes, pltpu.roll(flux_y, 64, 1), flux_z)
            for side, yz, x in ((parity, near, flux_x), (1 - parity, far, pltpu.roll(flux_x, 64, 1))):
                place = rows(s * PL + side * HALF, HALF)
                for lanes, value in ((slice(0, 128), yz), (slice(128, 256), x)):
                    high, low = halves(value)
                    bh[place, lanes] = high
                    bl[place, lanes] = low

        row = lax.broadcasted_iota(jnp.int32, (256, 128), 0)
        lane = lax.broadcasted_iota(jnp.int32, (256, 128), 1)
        for m in range(NX // 256):
            part = pl.ds(m * 256, 256)
            value = dot3(xb[0, part, :], xb[1, part, :], bh[...], bl[...])
            x = value[:, 128:]
            mode = (row // 2 + m * 128).astype(F32)
            sloped = jnp.where(row % 2 == 0, mode * pltpu.roll(x, 255, 0), -mode * pltpu.roll(x, 1, 0))
            send4[0, rows(chunk * NX + m * 256, 256), :] = value[:, :128] + jnp.where(lane < 64, sloped, 0.0)

        wide_send(send4, recv4, chunk, s4, r4, lambda peer: peer, plane(chunk))

    for copy in table_copies[5:]:
        copy.wait()

    @pl.loop(0, QL + 2)
    def _(i):
        pl.when(i < QL)(lambda: x_step(i))
        pl.when((i >= 1) & (i < QL + 1))(lambda: y_step(i - 1))
        pl.when(i >= 2)(lambda: x_back_step(i - 2))

    zh[...] = jnp.zeros_like(zh)
    zl[...] = jnp.zeros_like(zl)
    for c in range(QL):
        wait(recv4, c, NX, r4)
    wide_lanes = lax.broadcasted_iota(jnp.int32, (NZ, 128), 1) < 64

    @pl.loop(0, XL // 2)
    def _(i):
        for side in range(2):
            high, low = halves(recv4[0, pl.ds(2 * i + side, MZ, stride=XL), :])
            zh[:MZ, side * 128 : (side + 1) * 128] = high
            zl[:MZ, side * 128 : (side + 1) * 128] = low
        value = dot3(zb[0], zb[1], zh[...], zl[...])
        first = value[:NZ, :128] + pltpu.roll(value[NZ:, :128], 64, 1)
        second = pltpu.roll(value[:NZ, 128:], 64, 1) + value[NZ:, 128:]
        nonlinear = jnp.where(wide_lanes, first, second).T
        for side in range(2):
            buoyancy = b_ref[2 * i + side]
            right_side = buoyancy - (4.0 / NX) * nonlinear[side * YL : (side + 1) * YL]
            out_ref[2 * i + side] = right_side.astype(BF16)

    for c in range(QL):
        wait(send1, c, NX, s1)
        wait(send2, c, MX, s2, MX - PL)
        wait(send3, c, N * HALF, s3, (N - 1) * HALF)
        wait(send4, c, NX, s4)


def right_side_of(buoyancy, velocity_x, velocity_y, velocity_z):
    zf, xf, yf, yb, xb, zb = [jnp.asarray(t) for t in tables()]
    vmem = pl.BlockSpec(memory_space=pltpu.VMEM)
    hbm = pl.BlockSpec(memory_space=pltpu.HBM)
    fields = [pltpu.VMEM((XL, YL, NZ), F32)] * 4
    buffers = []
    for groups, count in ((2, QL * NX), (2, QL * MX), (3, QL * N * HALF), (1, QL * NX)):
        buffers += [pltpu.VMEM((groups, count, 128), F32)] * 2
    split = []
    for shape in ((NX, 256), (4 * PL, NY), (3 * PL, MY), (MX, 256), (256, 256)):
        split += [pltpu.VMEM(shape, BF16)] * 2
    sems = [pltpu.SemaphoreType.DMA((count,)) for count in (10,) + (QL,) * 8]
    return pl.pallas_call(
        kernel,
        out_shape=jax.ShapeDtypeStruct((XL, YL, NZ), BF16),
        in_specs=[hbm] * 10,
        out_specs=vmem,
        scratch_shapes=buffers + fields + [pltpu.VMEM(t.shape, BF16) for t in (zf, zb, xf, yf, yb, xb)] + split + sems,
        compiler_params=pltpu.CompilerParams(
            collective_id=1, has_side_effects=True, vmem_limit_bytes=55 * 1024 * 1024
        ),
        name="spectral",
    )(velocity_x, velocity_y, velocity_z, buoyancy, zf, zb, xf, yf, yb, xb)


def per_device(buoyancy, velocity_x, velocity_y, velocity_z, inverse_blocks):
    right_side = right_side_of(buoyancy, velocity_x, velocity_y, velocity_z)
    grouped = right_side.reshape(XL // 2, 2, YL // 2, 2, NZ)
    solved = jnp.einsum(
        "xyin,xaybn->xaybi", inverse_blocks, grouped, preferred_element_type=F32
    )
    return solved.reshape(XL, YL, NZ)


def solution(mesh):
    fields = P("wide", "narrow", None)
    return jax.shard_map(
        per_device,
        mesh=mesh,
        in_specs=(fields, fields, fields, fields, P("wide", "narrow", None, None)),
        out_specs=fields,
        check_vma=False,
    )
```

```python
import functools

import jax
import jax.numpy as jnp
import ml_dtypes
import numpy as np
from jax import lax
from jax.experimental import pallas as pl
from jax.experimental.pallas import tpu as pltpu
from jax.sharding import PartitionSpec as P

NX = 512
NY = 512
NZ = 128
MX = 768
MY = 768
MZ = 192
W = 32
N = 8
XL = NX // W
YL = NY // N
QL = MZ // W
PL = MX // N
HALF = PL // 2
F32 = jnp.float32
BF16 = jnp.bfloat16
MESH = pl.DeviceIdType.MESH


def fourier_table(n_coef, n_grid):
    index = np.arange(n_coef)
    phase = (index[:, None] // 2 * np.arange(n_grid)[None, :] % n_grid) * (2.0 * np.pi / n_grid)
    return np.where((index % 2 == 0)[:, None], np.cos(phase), np.sin(phase))


def fourier_inverse(n_coef, n_grid):
    index = np.arange(n_coef)
    modes = index // 2
    weight = np.where(modes == 0, np.where(index % 2 == 0, 1.0 / n_grid, 0.0), 2.0 / n_grid)
    return fourier_table(n_coef, n_grid).T * weight[None, :]


def cheb_table(n_coef, n_grid):
    orders = np.arange(n_coef)
    points = np.arange(n_grid)
    index_grid = orders[:, None] * (2 * points[None, :] + 1) % (4 * n_grid)
    return np.cos(index_grid * (np.pi / (2 * n_grid)))


def cheb_inverse(n_coef, n_grid):
    weight = np.where(np.arange(n_coef) == 0, 1.0 / n_grid, 2.0 / n_grid)
    return cheb_table(n_coef, n_grid).T * weight[None, :]


def cheb_slope(n_coef):
    rows = np.arange(n_coef)[:, None]
    cols = np.arange(n_coef)[None, :]
    inside = (cols > rows) & ((cols - rows) % 2 == 1)
    return np.where(inside, np.where(rows == 0, 1.0, 2.0) * cols, 0.0)


def split_table(table):
    high = table.astype(np.float32).astype(ml_dtypes.bfloat16)
    low = (table - high.astype(np.float64)).astype(np.float32).astype(ml_dtypes.bfloat16)
    return np.stack([high, low])


@functools.cache
def tables():
    z_forward = cheb_table(NZ, MZ).T.reshape(W, QL, NZ).transpose(1, 0, 2).reshape(MZ, NZ)
    x_forward = fourier_table(NX, MX).T
    y_forward = fourier_table(NY, MY)
    y_backward = fourier_inverse(NY, MY)
    x_backward = fourier_inverse(NX, MX).T
    plain = cheb_inverse(NZ, MZ)
    z_backward = np.zeros((2, NZ, 256))
    for i, source in enumerate((plain, plain @ cheb_slope(NZ).T)):
        z_backward[i, :, :MZ] = source.reshape(W, QL, NZ).transpose(2, 1, 0).reshape(NZ, MZ)
    z_backward = z_backward.reshape(2 * NZ, 256)
    return [split_table(t) for t in (z_forward, x_forward, y_forward, y_backward, x_backward, z_backward)]


def halves(value):
    high = value.astype(BF16)
    return high, (value - high.astype(F32)).astype(BF16)


def dot(a, b, dims=((1,), (0,))):
    return lax.dot_general(a, b, (dims, ((), ())), preferred_element_type=F32)


def dot3(a_high, a_low, b_high, b_low):
    return dot(a_high, b_high) + dot(a_low, b_high) + dot(a_high, b_low)


def rows(start, size):
    return pl.ds(pl.multiple_of(start, 16), size)


def kernel(
    vx_hbm, vy_hbm, vz_hbm, b_hbm, zf_hbm, zb_hbm, xf_hbm, yf_hbm, yb_hbm, xb_hbm,
    out_ref,
    send1, recv1, send2, recv2, send3, recv3, send4, recv4,
    vx_ref, vy_ref, vz_ref, b_ref, zf, zb, xf, yf, yb, xb,
    xh, xl, yh, yl, gh, gl, bh, bl, zh, zl, partial,
    table_sem, s1, r1, s2, r2, s3, r3, s4, r4,
):
    w = lax.axis_index("wide")
    n = lax.axis_index("narrow")
    across = lax.rem(n + 4, N)
    parity = lax.rem(n, 2)
    z_pos, rest = w // 4, lax.rem(w, 4)
    y_pos, x_pos = n // 4, lax.rem(n, 4)

    def wide_peer(k):
        step, turn = lax.rem(k, 8), k // 8
        away = (step + 1) // 2
        shift = jnp.where(lax.rem(step, 2) == 1, 4 - away, 4 + away)
        return lax.rem(z_pos + shift, 8) * 4 + lax.rem(rest + turn, 4)

    def narrow_peer(k):
        y_shift = jnp.where((k == 0) | (k == 2) | (k == 3) | (k == 6), 1, 0)
        x_shift = jnp.where(k < 2, 2, jnp.where(k == 6, 0, 1 + 2 * lax.rem(k, 2)))
        return lax.rem(y_pos + y_shift, 2) * 4 + lax.rem(x_pos + x_shift, 4)

    def flipped(wide):
        return wide + 2 - 4 * lax.rem(wide // 2, 2)

    def flips(wide, chunk):
        return lax.rem(wide + chunk, 2) == 1

    def plane(chunk):
        return jnp.where(flips(w, chunk) & (y_pos == 0), flipped(w), w)

    table_copies = [
        pltpu.make_async_copy(hbm, vmem, table_sem.at[i])
        for i, (hbm, vmem) in enumerate(
            (
                (vx_hbm, vx_ref), (vy_hbm, vy_ref), (vz_hbm, vz_ref), (b_hbm, b_ref), (zf_hbm, zf),
                (xf_hbm, xf), (yf_hbm, yf), (yb_hbm, yb), (xb_hbm, xb), (zb_hbm, zb),
            )
        )
    ]
    for copy in table_copies:
        copy.start()

    barrier = pltpu.get_barrier_semaphore()

    @pl.loop(0, W)
    def _(k):
        pl.semaphore_signal(barrier, inc=1, device_id=(wide_peer(k), across), device_id_type=MESH)

    for k in range(6):
        pl.semaphore_signal(barrier, inc=1, device_id=(w, narrow_peer(k)), device_id_type=MESH)
    for k in (0, 2, 3):
        pl.semaphore_signal(barrier, inc=1, device_id=(flipped(w), narrow_peer(k)), device_id_type=MESH)

    for copy in table_copies[:5]:
        copy.wait()
    odd = parity == 1

    def z_step(a, part, size):
        vx, vy, vz, b = vx_ref[a], vy_ref[a], vz_ref[a], b_ref[a]
        data = jnp.concatenate(
            [jnp.where(odd, vy, vx), jnp.where(odd, vx, vy), jnp.where(odd, b, vz), jnp.where(odd, vz, b)], axis=0
        )
        high, low = halves(data)
        nt = ((1,), (1,))
        first, second = zf[0, part : part + size], zf[1, part : part + size]
        value = dot(first, high, nt) + dot(second, high, nt) + dot(first, low, nt)
        for g in range(2):
            send1[g, pl.ds(part * XL + a, size, stride=XL), :] = value[:, g * 128 : (g + 1) * 128]

    @pl.loop(0, XL)
    def _(a):
        z_step(a, 0, W)

    pl.semaphore_wait(barrier, W + 9)

    def wide_send(src, dst, chunk, ssem, rsem, target, slot):
        @pl.loop(0, W)
        def _(k):
            peer = wide_peer(k)
            pltpu.make_async_remote_copy(
                src_ref=src.at[:, rows((chunk * W + peer) * XL, XL), :],
                dst_ref=dst.at[:, rows((chunk * W + slot) * XL, XL), :],
                send_sem=ssem.at[chunk],
                recv_sem=rsem.at[chunk],
                device_id=(target(peer), across),
                device_id_type=MESH,
            ).start()

    def narrow_send(src, dst, chunk, size, ssem, rsem, source_slot, target_slot):
        def block(slot):
            return rows((chunk * N + slot) * size, size)

        @pl.loop(0, N - 1)
        def _(k):
            peer = narrow_peer(k)
            wide = jnp.where(flips(w, chunk) & (peer // 4 != y_pos), flipped(w), w)
            pltpu.make_async_remote_copy(
                src_ref=src.at[:, block(source_slot(peer)), :],
                dst_ref=dst.at[:, block(target_slot), :],
                send_sem=ssem.at[chunk],
                recv_sem=rsem.at[chunk],
                device_id=(wide, peer),
                device_id_type=MESH,
            ).start()

        pltpu.make_async_copy(
            src.at[:, block(source_slot(n)), :], dst.at[:, block(target_slot), :], rsem.at[chunk]
        ).start()

    def wait(buffer, chunk, size, sem, part=None):
        ref = buffer.at[:, rows(chunk * size, part or size), :]
        pltpu.make_async_copy(ref, ref, sem.at[chunk]).wait()

    def forward(chunk):
        def holder(peer):
            return jnp.where(flips(peer, chunk) & (y_pos == 1), flipped(peer), peer)

        wide_send(send1, recv1, chunk, s1, r1, holder, w)

    forward(0)

    @pl.loop(0, XL)
    def _(a):
        z_step(a, W, MZ - W)

    @pl.loop(1, QL)
    def _(chunk):
        forward(chunk)

    low_lanes = lax.broadcasted_iota(jnp.int32, (PL, 128), 1) < 64
    half_lanes = lax.broadcasted_iota(jnp.int32, (HALF, 128), 1) < 64

    def x_step(chunk):
        wait(recv1, chunk, NX, r1)
        for g in range(2):
            high, low = halves(recv1[g, rows(chunk * NX, NX), :])
            xh[:, g * 128 : (g + 1) * 128] = high
            xl[:, g * 128 : (g + 1) * 128] = low

        @pl.loop(0, MX // 256)
        def _(m):
            part = rows(m * 256, 256)
            value = dot3(xf[0, part, :], xf[1, part, :], xh[...], xl[...])
            for g in range(2):
                send2[g, rows(chunk * MX + m * 256, 256), :] = value[:, g * 128 : (g + 1) * 128]

        narrow_send(send2, recv2, chunk, PL, s2, r2, lambda peer: peer, across)

    def y_step(chunk):
        wait(recv2, chunk, MX, r2)
        for g in range(2):
            for s in range(4):
                first = recv2[g, rows(chunk * MX + 2 * s * PL, PL), :]
                second = recv2[g, rows(chunk * MX + (2 * s + 1) * PL, PL), :]
                even = jnp.where(low_lanes, first, second)
                other = pltpu.roll(jnp.where(low_lanes, second, first), 64, 1)
                for f, value in ((2 * g, even), (2 * g + 1, other)):
                    high, low = halves(value)
                    yh[f * PL : (f + 1) * PL, s * 128 : (s + 1) * 128] = high
                    yl[f * PL : (f + 1) * PL, s * 128 : (s + 1) * 128] = low
        for j in range(MY // 256):
            cols = pl.ds(j * 256, 256)
            grid = dot3(yh[...], yl[...], yf[0, :, cols], yf[1, :, cols])
            for f in range(3):
                high, low = halves(grid[f * PL : (f + 1) * PL] * grid[3 * PL :])
                gh[f * PL : (f + 1) * PL, cols] = high
                gl[f * PL : (f + 1) * PL, cols] = low
        lane = lax.broadcasted_iota(jnp.int32, (PL, 128), 1)
        for j in range(NY // 256):
            cols = pl.ds(j * 256, 256)
            value = dot3(gh[...], gl[...], yb[0, :, cols], yb[1, :, cols])
            for f in range(3):
                for h in range(2):
                    part = value[f * PL : (f + 1) * PL, h * 128 : (h + 1) * 128]
                    if f == 1:
                        mode = (lane // 2 + (2 * j + h) * 64).astype(F32)
                        part = jnp.where(
                            lane % 2 == 0, mode * pltpu.roll(part, 127, 1), -mode * pltpu.roll(part, 1, 1)
                        )
                    first, second = part[:HALF], pltpu.roll(part[HALF:], 64, 1)
                    block = chunk * N + (2 * j + h) * 2
                    send3[f, rows(block * HALF, HALF), :] = jnp.where(half_lanes, first, second)
                    send3[f, rows((block + 1) * HALF, HALF), :] = jnp.where(half_lanes, second, first)
        narrow_send(send3, recv3, chunk, HALF, s3, r3, lambda peer: lax.rem(peer + 4, N), n)

    def x_back_step(chunk):
        wait(recv3, chunk, N * HALF, r3)
        for s in range(N):
            flux_x, flux_y, flux_z = (recv3[f, rows((chunk * N + s) * HALF, HALF), :] for f in range(3))
            near = jnp.where(half_lanes, flux_y, pltpu.roll(flux_z, 64, 1))
            far = jnp.where(half_lanes, pltpu.roll(flux_y, 64, 1), flux_z)
            for side, yz, x in ((parity, near, flux_x), (1 - parity, far, pltpu.roll(flux_x, 64, 1))):
                place = rows(s * PL + side * HALF, HALF)
                for lanes, value in ((slice(0, 128), yz), (slice(128, 256), x)):
                    high, low = halves(value)
                    bh[place, lanes] = high
                    bl[place, lanes] = low

        row = lax.broadcasted_iota(jnp.int32, (256, 128), 0)
        lane = lax.broadcasted_iota(jnp.int32, (256, 128), 1)
        for m in range(NX // 256):
            part = pl.ds(m * 256, 256)
            value = dot3(xb[0, part, :], xb[1, part, :], bh[...], bl[...])
            x = value[:, 128:]
            mode = (row // 2 + m * 128).astype(F32)
            sloped = jnp.where(row % 2 == 0, mode * pltpu.roll(x, 255, 0), -mode * pltpu.roll(x, 1, 0))
            send4[0, rows(chunk * NX + m * 256, 256), :] = value[:, :128] + jnp.where(lane < 64, sloped, 0.0)

        wide_send(send4, recv4, chunk, s4, r4, lambda peer: peer, plane(chunk))

    for copy in table_copies[5:]:
        copy.wait()

    @pl.loop(0, QL + 2)
    def _(i):
        pl.when(i < QL)(lambda: x_step(i))
        pl.when((i >= 1) & (i < QL + 1))(lambda: y_step(i - 1))
        pl.when(i >= 2)(lambda: x_back_step(i - 2))

    zh[...] = jnp.zeros_like(zh)
    zl[...] = jnp.zeros_like(zl)
    early = 4 * W

    def z_rows(i, start, size):
        for side in range(2):
            high, low = halves(recv4[0, pl.ds(start * XL + 2 * i + side, size, stride=XL), :])
            zh[start : start + size, side * 128 : (side + 1) * 128] = high
            zl[start : start + size, side * 128 : (side + 1) * 128] = low

    for c in range(4):
        wait(recv4, c, NX, r4)

    @pl.loop(0, XL // 2)
    def _(i):
        z_rows(i, 0, early)
        partial[i] = dot3(zb[0, :, :early], zb[1, :, :early], zh[:early, :], zl[:early, :])

    for c in range(4, QL):
        wait(recv4, c, NX, r4)
    wide_lanes = lax.broadcasted_iota(jnp.int32, (NZ, 128), 1) < 64

    @pl.loop(0, XL // 2)
    def _(i):
        z_rows(i, early, MZ - early)
        value = partial[i] + dot3(zb[0, :, early:], zb[1, :, early:], zh[early:, :], zl[early:, :])
        first = value[:NZ, :128] + pltpu.roll(value[NZ:, :128], 64, 1)
        second = pltpu.roll(value[:NZ, 128:], 64, 1) + value[NZ:, 128:]
        nonlinear = jnp.where(wide_lanes, first, second).T
        for side in range(2):
            buoyancy = b_ref[2 * i + side]
            right_side = buoyancy - (4.0 / NX) * nonlinear[side * YL : (side + 1) * YL]
            out_ref[2 * i + side] = right_side.astype(BF16)

    for c in range(QL):
        wait(send1, c, NX, s1)
        wait(send2, c, MX, s2, MX - PL)
        wait(send3, c, N * HALF, s3, (N - 1) * HALF)
        wait(send4, c, NX, s4)


def right_side_of(buoyancy, velocity_x, velocity_y, velocity_z):
    zf, xf, yf, yb, xb, zb = [jnp.asarray(t) for t in tables()]
    vmem = pl.BlockSpec(memory_space=pltpu.VMEM)
    hbm = pl.BlockSpec(memory_space=pltpu.HBM)
    fields = [pltpu.VMEM((XL, YL, NZ), F32)] * 4
    buffers = []
    for groups, count in ((2, QL * NX), (2, QL * MX), (3, QL * N * HALF), (1, QL * NX)):
        buffers += [pltpu.VMEM((groups, count, 128), F32)] * 2
    split = []
    for shape in ((NX, 256), (4 * PL, NY), (3 * PL, MY), (MX, 256), (256, 256)):
        split += [pltpu.VMEM(shape, BF16)] * 2
    split.append(pltpu.VMEM((XL // 2, 2 * NZ, 256), F32))
    sems = [pltpu.SemaphoreType.DMA((count,)) for count in (10,) + (QL,) * 8]
    return pl.pallas_call(
        kernel,
        out_shape=jax.ShapeDtypeStruct((XL, YL, NZ), BF16),
        in_specs=[hbm] * 10,
        out_specs=vmem,
        scratch_shapes=buffers + fields + [pltpu.VMEM(t.shape, BF16) for t in (zf, zb, xf, yf, yb, xb)] + split + sems,
        compiler_params=pltpu.CompilerParams(
            collective_id=1, has_side_effects=True, vmem_limit_bytes=55 * 1024 * 1024
        ),
        name="spectral",
    )(velocity_x, velocity_y, velocity_z, buoyancy, zf, zb, xf, yf, yb, xb)


def per_device(buoyancy, velocity_x, velocity_y, velocity_z, inverse_blocks):
    right_side = right_side_of(buoyancy, velocity_x, velocity_y, velocity_z)
    grouped = right_side.reshape(XL // 2, 2, YL // 2, 2, NZ)
    solved = jnp.einsum(
        "xyin,xaybn->xaybi", inverse_blocks, grouped, preferred_element_type=F32
    )
    return solved.reshape(XL, YL, NZ)


def solution(mesh):
    fields = P("wide", "narrow", None)
    return jax.shard_map(
        per_device,
        mesh=mesh,
        in_specs=(fields, fields, fields, fields, P("wide", "narrow", None, None)),
        out_specs=fields,
        check_vma=False,
    )
```
